256 devices in a mesh: dp: 32 (over z_lo, x, y), tensor: 8 (over z_hi, core).
Axes of the slice: x: 4, y: 4, z: 8 (z_hi: 4, z_lo: 2; z = z_hi * 2 + z_lo), core: 2. Of those that a mesh axis runs over, the one named last changes fastest.
Arguments:
- activations: bfloat16 [8192, 14336], P('dp', 'tensor'), may hold values from -6 to 6
- out_grads: bfloat16 [8192, 4096], P('dp', 'tensor'), may hold values from -0.06591797 to 0.06591797
Outputs:
- fisher: float32 [14336, 4096], P('tensor', 'dp')
The draws below stay inside these ranges and needn't reach their ends.
All inputs are finite; a program needn't handle non-finite values.
Results may differ from the reference program's by a relative error of at most 0.0003.
Values may be sent and summed in bfloat16 or wider, within the bound.
No kernel may reach another device: no remote copies, remote signals or barrier semaphores. Data moves between devices by JAX's collectives and lax.ppermute only.
A program may use at most 192 MiB of HBM per device.

```python
import jax
import jax.numpy as jnp
from jax import lax

FF = 14336
D = 4096
LEN = 128
SEQ_DEV = 2
SEQS = 64
TOKENS = 8192
N_DP = 32


def spiked(result, rng, source, target, shards_of, factor):
    def block_of(dim):
        return (jnp.arange(result.shape[dim]) // (result.shape[dim] // shards_of)).reshape((-1,) + (1,) * (result.ndim - 1 - dim))

    first = jax.random.permutation(rng, shards_of)[block_of(target)]
    far = (block_of(target) + shards_of // 2) % shards_of
    return jnp.where((block_of(source) == first) | (block_of(source) == far), factor * result, result)


def level_of(own_key, extent, split, least, top_value):
    level = 1.0
    for position, blocks in split:
        heights = jax.random.uniform(jax.random.fold_in(jax.random.fold_in(own_key, 6), position), (blocks,), jnp.float32, least / len(split), top_value / len(split))
        level = level * jnp.repeat(jnp.exp(heights), extent[position] // blocks).reshape((-1,) + (1,) * (len(extent) - 1 - position))
    return level


def centred(key, shape, scale, reach, split=(), held_as=jnp.bfloat16):
    drawn = scale * jax.random.normal(key, shape, jnp.float32)
    if split:
        drawn = drawn * level_of(key, shape, split, -0.22, 0.18)
    return jnp.clip(drawn, -reach, reach).astype(held_as)


def gaussian_with(key, extent, deviation, limit, cuts, heavy, held_as=jnp.bfloat16):
    entries = deviation * jax.random.normal(key, extent, jnp.float32)
    if cuts:
        entries = entries * level_of(key, extent, cuts, -0.22, 0.18)
    return jnp.clip(spiked(entries, jax.random.fold_in(key, 3), *heavy), -limit, limit).astype(held_as)


def setup_inputs(seed: int = 0) -> dict:
    key_list = jax.random.split(jax.random.key(seed), 3)
    return {
        "activations": centred(key_list[0], (TOKENS, FF), 1.0, 6.0, ((0, 32), (1, 8))),
        "out_grads": gaussian_with(key_list[1], (TOKENS, D), ((LEN * SEQS) ** -0.5), 0.06591797, ((0, 32), (1, 8)), (0, 1, 32, 2.75)),
    }


def group_partial(inputs_group, grads_group):
    def add_sequence(total, pair):
        grads = jnp.dot(pair[0].T, pair[1], preferred_element_type=jnp.float32)
        return total + grads * grads, None

    start = jnp.zeros((FF, D), jnp.float32)
    total, unused = lax.scan(add_sequence, start, (inputs_group, grads_group))
    return total


def reference(activations, out_grads):
    inputs_all = activations.reshape(N_DP, SEQ_DEV, LEN, FF)
    grads_all = out_grads.reshape(N_DP, SEQ_DEV, LEN, D)

    def add_group(fisher, pair):
        return fisher + group_partial(pair[0], pair[1]), None

    fisher, unused = lax.scan(add_group, jnp.zeros((FF, D), jnp.float32), (inputs_all, grads_all))
    return fisher
```

```python
import functools

import jax
import jax.numpy as jnp
from jax import lax
from jax.experimental import pallas as pl
from jax.experimental.pallas import tpu as pltpu
from jax.sharding import PartitionSpec as P

LEN = 128
NX, NY, NZ = 4, 4, 4
TILE = 256
CHUNKS = (768, 512, 512)
CODE_TOP = 2.0**14
LEAST = 2.0**-120
VMEM = 48 * 1024 * 1024


def dp_index(z, x, y):
    return (z % 2) * NX * NY + (x % NX) * NY + (y % NY)


def dp_moves(dz, dx, dy):
    return [
        (dp_index(z, x, y), dp_index(z + dz, x + dx, y + dy))
        for z in range(2)
        for x in range(NX)
        for y in range(NY)
    ]


def tensor_moves(dz, flip):
    return [
        (2 * z + c, 2 * ((z + dz) % NZ) + (c ^ flip))
        for z in range(NZ)
        for c in range(2)
    ]


def from_y(array, offset):
    return lax.ppermute(array, "dp", dp_moves(0, 0, -offset))


def to_x(array, offset):
    return lax.ppermute(array, "dp", dp_moves(0, offset, 0))


def to_z_lo(array):
    return lax.ppermute(array, "dp", dp_moves(1, 0, 0))


def from_z(array, offset):
    return lax.ppermute(array, "tensor", tensor_moves(-offset, 0))


def from_core(array):
    return lax.ppermute(array, "tensor", tensor_moves(0, 1))


def encode(total):
    top = jnp.max(total, axis=0, keepdims=True)
    top = jnp.maximum(top, LEAST).astype(jnp.bfloat16).astype(jnp.float32)
    scaled = total * (1.0 / top) * CODE_TOP
    scaled = scaled * scaled
    scaled = scaled * scaled
    scaled = scaled * scaled
    return scaled.astype(jnp.bfloat16), top


def decode(code, top):
    value = jnp.maximum(code.astype(jnp.float32), 2.0**-126)
    return jnp.exp(jnp.log(value) * 0.125) * (top * (1.0 / CODE_TOP))


def put_one(ref, total):
    code, top = encode(total)
    ref[:LEN, :] = code
    ref[LEN:, :] = jnp.broadcast_to(top, (16, top.shape[1])).astype(jnp.bfloat16)


def put_two(ref, first, second):
    code_0, top_0 = encode(first)
    code_1, top_1 = encode(second)
    ref[:LEN, :] = code_0
    ref[LEN : 2 * LEN, :] = code_1
    shape = (8, top_0.shape[1])
    tops = jnp.concatenate(
        [jnp.broadcast_to(top_0, shape), jnp.broadcast_to(top_1, shape)], axis=0
    )
    ref[2 * LEN :, :] = tops.astype(jnp.bfloat16)


def get_one(ref):
    tops = ref[LEN:, :].astype(jnp.float32)
    return decode(ref[:LEN, :], tops[:1])


def get_two(ref, which):
    tops = ref[2 * LEN :, :].astype(jnp.float32)
    return decode(ref[which * LEN : (which + 1) * LEN, :], tops[8 * which : 8 * which + 1])


def partial_kernel(
    slots, a_0, a_1, a_2a, a_2b, a_3, grads, own, keep_up, keep_down, up, down
):
    def total_of(k, j):
        block = slots[4 * j + k]
        total = None
        for o, pair in enumerate(
            (
                (a_0[:LEN, :], a_0[LEN:, :]),
                (a_1[:LEN, :], a_1[LEN:, :]),
                (a_2a[...], a_2b[...]),
                (a_3[:LEN, :], a_3[LEN:, :]),
            )
        ):
            for s in range(2):
                found = jnp.dot(
                    grads[block, o, :, s * LEN : (s + 1) * LEN],
                    pair[s],
                    preferred_element_type=jnp.float32,
                )
                total = found * found if total is None else total + found * found
        return total

    put_two(up, total_of(2, 0), total_of(1, 1))
    put_two(down, total_of(2, 1), total_of(3, 0))
    keep_up[...] = total_of(1, 0)
    keep_down[...] = total_of(3, 1)
    own[:LEN, :] = total_of(0, 0)
    own[LEN:, :] = total_of(0, 1)


def call(body, name, features, tall_in, tall_out, flops):
    in_bytes = sum(h * features * (2 if t == jnp.bfloat16 else 4) for h, t in tall_in)
    out_bytes = sum(h * features * (2 if t == jnp.bfloat16 else 4) for h, t in tall_out)
    return pl.pallas_call(
        body,
        name=name,
        grid=(features // TILE,),
        in_specs=[pl.BlockSpec((h, TILE), lambda i: (0, i)) for h, _ in tall_in],
        out_specs=[pl.BlockSpec((h, TILE), lambda i: (0, i)) for h, _ in tall_out],
        out_shape=[jax.ShapeDtypeStruct((h, features), t) for h, t in tall_out],
        compiler_params=pltpu.CompilerParams(vmem_limit_bytes=VMEM),
        cost_estimate=pl.CostEstimate(
            flops=flops, bytes_accessed=in_bytes + out_bytes, transcendentals=0
        ),
    )


def partial_sums(slots, acts, grads):
    features = acts[0].shape[1]
    f32, b16 = jnp.float32, jnp.bfloat16
    outs = ((2 * LEN, f32), (LEN, f32), (LEN, f32), (2 * LEN + 16, b16), (2 * LEN + 16, b16))
    return pl.pallas_call(
        partial_kernel,
        name="partial_sums",
        grid_spec=pltpu.PrefetchScalarGridSpec(
            num_scalar_prefetch=1,
            grid=(features // TILE,),
            in_specs=[
                pl.BlockSpec((a.shape[0], TILE), lambda i, s: (0, i)) for a in acts
            ]
            + [pl.BlockSpec(grads.shape, lambda i, s: (0, 0, 0, 0))],
            out_specs=[pl.BlockSpec((h, TILE), lambda i, s: (0, i)) for h, _ in outs],
        ),
        out_shape=[jax.ShapeDtypeStruct((h, features), t) for h, t in outs],
        compiler_params=pltpu.CompilerParams(vmem_limit_bytes=VMEM),
        cost_estimate=pl.CostEstimate(
            flops=2 * 1024 * 1024 * features, bytes_accessed=2**21, transcendentals=0
        ),
    )(slots, *acts, grads)


def relay_kernel(keep_up, keep_down, from_down, from_up, up, down):
    put_one(up, keep_up[...] + get_two(from_down, 0))
    put_one(down, keep_down[...] + get_two(from_up, 0))


def gather_kernel(own, from_down, from_up, late_down, late_up, kept, sent):
    kept[...] = own[:LEN, :] + (get_two(from_up, 1) + get_one(late_down))
    put_one(sent, own[LEN:, :] + (get_two(from_down, 1) + get_one(late_up)))


def final_kernel(kept, received, out):
    out[...] = (kept[...] + get_one(received)).T


def final(kept, received):
    features = kept.shape[1]
    return pl.pallas_call(
        final_kernel,
        name="final",
        grid=(features // TILE,),
        in_specs=[
            pl.BlockSpec((LEN, TILE), lambda i: (0, i)),
            pl.BlockSpec((LEN + 16, TILE), lambda i: (0, i)),
        ],
        out_specs=pl.BlockSpec((TILE, LEN), lambda i: (i, 0)),
        out_shape=jax.ShapeDtypeStruct((features, LEN), jnp.float32),
        compiler_params=pltpu.CompilerParams(vmem_limit_bytes=VMEM),
    )(kept, received)


def gather_grads(out_grads, y):
    turned = out_grads.T
    width = turned.shape[0] // NY

    def block_for(offset):
        start = ((y + offset) % NY) * width
        return lax.dynamic_slice_in_dim(turned, start, width, axis=0)

    mine = jnp.stack(
        [block_for(0)] + [from_y(block_for(-o), o) for o in range(1, NY)]
    )
    z_up = from_z(mine, 1)
    z_down = from_z(mine, -1)
    far = jnp.concatenate([from_z(z_down[:2], -1), from_z(z_up[2:], 1)])
    near = jnp.stack([z_up, z_down])
    other_mine = from_core(mine)
    other_near = from_core(near)
    other_far = from_core(far)
    return jnp.stack(
        [mine, other_mine, z_up, other_near[0], far, other_far, z_down, other_near[1]]
    )


def gather_acts(chunk):
    after = from_y(chunk, 1)
    before = from_y(chunk, -1)
    far_a = from_y(before[:LEN], -1)
    far_b = from_y(after[LEN:], 1)
    return chunk, after, far_a, far_b, before


def per_device(activations, out_grads):
    f32, b16 = jnp.float32, jnp.bfloat16
    dp, tensor = lax.axis_index("dp"), lax.axis_index("tensor")
    z_lo, x, y = dp // (NX * NY), (dp // NY) % NX, dp % NY
    z_hi, core = tensor // 2, tensor % 2
    slots = []
    for j in range(2):
        for k in range(NX):
            wanted = ((z_lo + j) % 2) * NX + (x + k) % NX
            slots.append(((wanted // 2 - z_hi) % NZ) * 2 + (wanted + core) % 2)
    slots = jnp.stack(slots).astype(jnp.int32)

    grads = gather_grads(out_grads, y)
    starts = [sum(CHUNKS[:i]) for i in range(len(CHUNKS))]
    results = []
    for start, size in zip(starts, CHUNKS, strict=True):
        acts = gather_acts(activations[:, start : start + size])
        own, keep_up, keep_down, up, down = partial_sums(slots, acts, grads)
        from_down, from_up = to_x(up, 1), to_x(down, -1)
        one, two = LEN + 16, 2 * LEN + 16
        up, down = call(
            relay_kernel,
            "relay",
            size,
            ((LEN, f32), (LEN, f32), (two, b16), (two, b16)),
            ((one, b16), (one, b16)),
            16 * LEN * size,
        )(keep_up, keep_down, from_down, from_up)
        late_down, late_up = to_x(up, 1), to_x(down, -1)
        kept, sent = call(
            gather_kernel,
            "gather",
            size,
            ((2 * LEN, f32), (two, b16), (two, b16), (one, b16), (one, b16)),
            ((LEN, f32), (one, b16)),
            32 * LEN * size,
        )(own, from_down, from_up, late_down, late_up)
        results.append(final(kept, to_z_lo(sent)))
    return jnp.concatenate(results)


def solution(mesh):
    in_specs = (P("dp", "tensor"), P("dp", "tensor"))
    out_specs = P("tensor", "dp")
    return jax.shard_map(
        per_device, mesh=mesh, in_specs=in_specs, out_specs=out_specs, check_vma=False
    )
```

```python
import functools

import jax
import jax.numpy as jnp
from jax import lax
from jax.experimental import pallas as pl
from jax.experimental.pallas import tpu as pltpu
from jax.sharding import PartitionSpec as P

LEN = 128
NX, NY, NZ = 4, 4, 4
TILE = 256
LANES = 128
CHUNKS = ((512, "abz"), (512, "baz"), (512, "zab"), (256, "abz"))
CODE_TOP = 2.0**14
LEAST = 2.0**-120
VMEM = 16 * 1024 * 1024


def dp_index(z, x, y):
    return (z % 2) * NX * NY + (x % NX) * NY + (y % NY)


def swap(array, z=0, x=0, y=0):
    pairs = [
        (dp_index(k, i, j), dp_index(k ^ z, i ^ x, j ^ y))
        for k in range(2)
        for i in range(NX)
        for j in range(NY)
    ]
    return lax.ppermute(array, "dp", pairs)


FOLDS = {"z": {"z": 1}, "a": {"x": 1}, "b": {"x": 3}}


def tensor_moves(dz, flip):
    return [
        (2 * z + c, 2 * ((z + dz) % NZ) + (c ^ flip))
        for z in range(NZ)
        for c in range(2)
    ]


def from_y(array, offset):
    pairs = [
        (dp_index(k, i, j), dp_index(k, i, j - offset))
        for k in range(2)
        for i in range(NX)
        for j in range(NY)
    ]
    return lax.ppermute(array, "dp", pairs)


def from_z(array, offset):
    return lax.ppermute(array, "tensor", tensor_moves(-offset, 0))


def from_core(array):
    return lax.ppermute(array, "tensor", tensor_moves(0, 1))


def after(later, *earlier):
    return lax.optimization_barrier((later, *earlier))[0]


def put(ref, parts):
    pieces = [p[:, n : n + LANES] for p in parts for n in range(0, TILE, LANES)]
    tops = [jnp.max(p, axis=0, keepdims=True) for p in pieces]
    top = functools.reduce(jnp.maximum, tops)
    top = jnp.maximum(top, LEAST).astype(jnp.bfloat16).astype(jnp.float32)
    inverse = 1.0 / top
    row = 0
    for piece in pieces:
        scaled = piece * inverse * CODE_TOP
        scaled = scaled * scaled
        scaled = scaled * scaled
        scaled = scaled * scaled
        ref[0, row : row + piece.shape[0], :] = scaled.astype(jnp.bfloat16)
        row += piece.shape[0]
    ref[0, row:, :] = jnp.broadcast_to(top, (16, LANES)).astype(jnp.bfloat16)


def get(ref, start, rows):
    scale = ref[0, -16:, :].astype(jnp.float32)[:1] * (1.0 / CODE_TOP)
    found = []
    for n in range(TILE // LANES):
        code = ref[0, start + n * rows : start + (n + 1) * rows, :]
        value = jnp.maximum(code.astype(jnp.float32), 2.0**-126)
        found.append(jnp.exp(jnp.log(value) * 0.125) * scale)
    return jnp.concatenate(found, axis=1)


def message(rows, features):
    return (features // TILE, rows * (TILE // LANES) + 16, LANES)


def squares(slot, grads, acts):
    own, after_y, far_a, far_b, before_y = acts
    total = None
    for e, pair in enumerate(
        (
            (own[:LEN, :], own[LEN:, :]),
            (after_y[:LEN, :], after_y[LEN:, :]),
            (far_a[...], far_b[...]),
            (before_y[:LEN, :], before_y[LEN:, :]),
        )
    ):
        for s in range(2):
            found = jnp.dot(
                grads[slot, e, :, s * LEN : (s + 1) * LEN],
                pair[s],
                preferred_element_type=jnp.float32,
            )
            total = found * found if total is None else total + found * found
    return total


def sums_kernel(run, slots, *refs):
    *acts, grads, kept, sent = refs
    put(sent, [squares(slots[8 * run + n], grads, acts) for n in range(4, 8)])
    for n in range(4):
        block = squares(slots[8 * run + n], grads, acts)
        kept[n * LEN : (n + 1) * LEN, :] = block


def fold_kernel(slots, mine, received, kept, sent):
    half = kept.shape[0] // LEN
    rows = LEN * (TILE // LANES)

    def block(n):
        return mine[n * LEN : (n + 1) * LEN, :] + get(received, n * rows, LEN)

    put(sent, [block(n) for n in range(half, 2 * half)])
    for n in range(half):
        kept[n * LEN : (n + 1) * LEN, :] = block(n)


def final_kernel(mine, received, *refs):
    refs[-1][...] = (mine[...] + get(received, 0, LEN)).T


def spec_of(shape, start):
    if len(shape) == 3:
        return pl.BlockSpec((1,) + shape[1:], lambda i, s: (i, 0, 0))
    return pl.BlockSpec((shape[0], TILE), lambda i, s: (0, i + start))


def call(body, name, features, scalars, ins, outs, cost):
    return pl.pallas_call(
        body,
        name=name,
        grid_spec=pltpu.PrefetchScalarGridSpec(
            num_scalar_prefetch=1,
            grid=(features // TILE,),
            in_specs=[
                pl.BlockSpec(a.shape, lambda i, s: (0, 0, 0, 0))
                if a.ndim == 4
                else spec_of(a.shape, start)
                for a, start in ins
            ],
            out_specs=[spec_of(shape, 0) for shape, _ in outs],
        ),
        out_shape=[jax.ShapeDtypeStruct(shape, dtype) for shape, dtype in outs],
        compiler_params=pltpu.CompilerParams(vmem_limit_bytes=VMEM),
        cost_estimate=pl.CostEstimate(
            flops=cost, bytes_accessed=1, transcendentals=0
        ),
    )(scalars, *[a for a, _ in ins])


def sums(run, slots, acts, grads, start, features):
    outs = (
        ((4 * LEN, features), jnp.float32),
        (message(4 * LEN, features), jnp.bfloat16),
    )
    ins = [(a, start // TILE) for a in acts] + [(grads, 0)]
    cost = 2 * 1024 * 1024 * features
    body = functools.partial(sums_kernel, run)
    return call(body, "sums", features, slots, ins, outs, cost)


def fold(slots, mine, received):
    rows, features = mine.shape[0] // 2, mine.shape[1]
    outs = (
        ((rows, features), jnp.float32),
        (message(rows, features), jnp.bfloat16),
    )
    return call(fold_kernel, "fold", features, slots, [(mine, 0), (received, 0)], outs, 1)


def final(mine, received, start, total, before):
    first = start // TILE
    ins = (mine, received) if before is None else (mine, received, before)
    specs = [
        pl.BlockSpec((LEN, TILE), lambda i: (0, i)),
        pl.BlockSpec((1,) + received.shape[1:], lambda i: (i, 0, 0)),
        pl.BlockSpec(memory_space=pl.ANY),
    ]
    return pl.pallas_call(
        final_kernel,
        name="final",
        grid=(mine.shape[1] // TILE,),
        in_specs=specs[: len(ins)],
        out_specs=pl.BlockSpec((TILE, LEN), lambda i: (i + first, 0)),
        out_shape=jax.ShapeDtypeStruct((total, LEN), jnp.float32),
        input_output_aliases={} if before is None else {2: 0},
        compiler_params=pltpu.CompilerParams(vmem_limit_bytes=VMEM),
    )(*ins)


def per_device(activations, out_grads):
    dp, tensor = lax.axis_index("dp"), lax.axis_index("tensor")
    z_lo, x, y = dp // (NX * NY), (dp // NY) % NX, dp % NY
    z_hi, core = tensor // 2, tensor % 2

    def slots_of(order):
        slots = []
        for n in range(8):
            bits = {d: (n >> (2 - i)) & 1 for i, d in enumerate(order)}
            wanted = (z_lo ^ bits["z"]) * NX + (x ^ bits["a"] ^ (3 * bits["b"]))
            slots.append(((wanted // 2 - z_hi) % NZ) * 2 + (wanted + core) % 2)
        return slots

    slots = [slot for _, order in CHUNKS for slot in slots_of(order)]
    slots = jnp.stack(slots).astype(jnp.int32)
    turned = out_grads.T
    width = turned.shape[0] // NY

    def block_for(offset):
        start = ((y + offset) % NY) * width
        return lax.dynamic_slice_in_dim(turned, start, width, axis=0)

    mine = jnp.stack([block_for(0)] + [from_y(block_for(-o), o) for o in range(1, NY)])
    mine, slots = lax.optimization_barrier((mine, slots))
    after_y, before_y = from_y(activations, 1), from_y(activations, -1)
    z_up, z_down = from_z(mine, 1), from_z(mine, -1)
    other_mine = from_core(mine)
    near = jnp.stack([z_up, z_down])
    far = jnp.concatenate([from_z(near[1, :2], -1), from_z(near[0, 2:], 1)])
    far_a, far_b = from_y(before_y[:LEN], -1), from_y(after_y[LEN:], 1)
    other_near = from_core(near)
    far = after(far, far_a, far_b)
    other_far = from_core(far)
    grads = jnp.stack(
        [mine, other_mine, near[0], other_near[0]]
        + [far, other_far, near[1], other_near[1]]
    )
    acts = (activations, after_y, far_a, far_b, before_y)

    start, runs = 0, []
    for run, (features, order) in enumerate(CHUNKS):
        kept, sent = sums(run, slots, acts, grads, start, features)
        slots = after(slots, kept)
        runs.append((start, order, kept, swap(sent, **FOLDS[order[0]])))
        start += features
    for step in (1, 2):
        for n, (first, order, kept, received) in enumerate(runs):
            kept, sent = fold(slots, kept, received)
            slots = after(slots, kept)
            received = swap(sent, **FOLDS[order[step]])
            runs[n] = (first, order, kept, received)
    result = None
    for first, _, kept, received in runs:
        result = final(kept, received, first, start, result)
    return result


def solution(mesh):
    in_specs = (P("dp", "tensor"), P("dp", "tensor"))
    out_specs = P("tensor", "dp")
    return jax.shard_map(
        per_device, mesh=mesh, in_specs=in_specs, out_specs=out_specs, check_vma=False
    )
```

```python
import functools

import jax
import jax.numpy as jnp
from jax import lax
from jax.experimental import pallas as pl
from jax.experimental.pallas import tpu as pltpu
from jax.sharding import PartitionSpec as P

LEN = 128
NX, NY, NZ = 4, 4, 4
TILE = 256
LANES = 128
CHUNKS = ((512, "abz"), (512, "baz"), (512, "zab"), (256, "abz"))
CODE_TOP = 2.0**14
LEAST = 2.0**-120
VMEM = 16 * 1024 * 1024


def dp_index(z, x, y):
    return (z % 2) * NX * NY + (x % NX) * NY + (y % NY)


def swap(array, z=0, x=0, y=0):
    pairs = [
        (dp_index(k, i, j), dp_index(k ^ z, i ^ x, j ^ y))
        for k in range(2)
        for i in range(NX)
        for j in range(NY)
    ]
    return lax.ppermute(array, "dp", pairs)


FOLDS = {"z": {"z": 1}, "a": {"x": 1}, "b": {"x": 3}}


def tensor_moves(dz, flip):
    return [
        (2 * z + c, 2 * ((z + dz) % NZ) + (c ^ flip))
        for z in range(NZ)
        for c in range(2)
    ]


def from_y(array, offset):
    pairs = [
        (dp_index(k, i, j), dp_index(k, i, j - offset))
        for k in range(2)
        for i in range(NX)
        for j in range(NY)
    ]
    return lax.ppermute(array, "dp", pairs)


def from_z(array, offset):
    return lax.ppermute(array, "tensor", tensor_moves(-offset, 0))


def from_core(array):
    return lax.ppermute(array, "tensor", tensor_moves(0, 1))


def after(later, *earlier):
    return lax.optimization_barrier((later, *earlier))[0]


def put(ref, parts):
    pieces = [p[:, n : n + LANES] for p in parts for n in range(0, TILE, LANES)]
    tops = [jnp.max(p, axis=0, keepdims=True) for p in pieces]
    top = functools.reduce(jnp.maximum, tops)
    top = jnp.maximum(top, LEAST).astype(jnp.bfloat16).astype(jnp.float32)
    inverse = 1.0 / top
    row = 0
    for piece in pieces:
        scaled = piece * inverse * CODE_TOP
        scaled = scaled * scaled
        scaled = scaled * scaled
        scaled = scaled * scaled
        ref[0, row : row + piece.shape[0], :] = scaled.astype(jnp.bfloat16)
        row += piece.shape[0]
    ref[0, row:, :] = jnp.broadcast_to(top, (16, LANES)).astype(jnp.bfloat16)


def get(ref, start, rows):
    scale = ref[0, -16:, :].astype(jnp.float32)[:1] * (1.0 / CODE_TOP)
    found = []
    for n in range(TILE // LANES):
        code = ref[0, start + n * rows : start + (n + 1) * rows, :]
        value = jnp.maximum(code.astype(jnp.float32), 2.0**-126)
        found.append(jnp.exp(jnp.log(value) * 0.125) * scale)
    return jnp.concatenate(found, axis=1)


def message(rows, features):
    return (features // TILE, rows * (TILE // LANES) + 16, LANES)


def squares(slot, grads, acts):
    own, after_y, far_a, far_b, before_y = acts
    total = None
    for e, pair in enumerate(
        (
            (own[:LEN, :], own[LEN:, :]),
            (after_y[:LEN, :], after_y[LEN:, :]),
            (far_a[...], far_b[...]),
            (before_y[:LEN, :], before_y[LEN:, :]),
        )
    ):
        for s in range(2):
            found = jnp.dot(
                grads[slot, e, :, s * LEN : (s + 1) * LEN],
                pair[s],
                preferred_element_type=jnp.float32,
            )
            total = found * found if total is None else total + found * found
    return total


def sent_kernel(run, slots, *refs):
    *acts, grads, sent = refs
    put(sent, [squares(slots[8 * run + n], grads, acts) for n in range(4, 8)])


def kept_kernel(run, slots, *refs):
    *acts, grads, kept = refs
    for n in range(4):
        block = squares(slots[8 * run + n], grads, acts)
        kept[n * LEN : (n + 1) * LEN, :] = block


def fold_kernel(slots, mine, received, kept, sent):
    half = kept.shape[0] // LEN
    rows = LEN * (TILE // LANES)

    def block(n):
        return mine[n * LEN : (n + 1) * LEN, :] + get(received, n * rows, LEN)

    put(sent, [block(n) for n in range(half, 2 * half)])
    for n in range(half):
        kept[n * LEN : (n + 1) * LEN, :] = block(n)


def final_kernel(mine, received, *refs):
    refs[-1][...] = (mine[...] + get(received, 0, LEN)).T


def spec_of(shape, start):
    if len(shape) == 3:
        return pl.BlockSpec((1,) + shape[1:], lambda i, s: (i, 0, 0))
    return pl.BlockSpec((shape[0], TILE), lambda i, s: (0, i + start))


def call(body, name, features, scalars, ins, outs, cost):
    return pl.pallas_call(
        body,
        name=name,
        grid_spec=pltpu.PrefetchScalarGridSpec(
            num_scalar_prefetch=1,
            grid=(features // TILE,),
            in_specs=[
                pl.BlockSpec(a.shape, lambda i, s: (0, 0, 0, 0))
                if a.ndim == 4
                else spec_of(a.shape, start)
                for a, start in ins
            ],
            out_specs=[spec_of(shape, 0) for shape, _ in outs],
        ),
        out_shape=[jax.ShapeDtypeStruct(shape, dtype) for shape, dtype in outs],
        compiler_params=pltpu.CompilerParams(vmem_limit_bytes=VMEM),
        cost_estimate=pl.CostEstimate(
            flops=cost, bytes_accessed=1, transcendentals=0
        ),
    )(scalars, *[a for a, _ in ins])


def sums(body, name, run, slots, acts, grads, start, out):
    features = CHUNKS[run][0]
    ins = [(a, start // TILE) for a in acts] + [(grads, 0)]
    cost = 1024 * 1024 * features
    body = functools.partial(body, run)
    return call(body, name, features, slots, ins, (out,), cost)[0]


def sent_sums(run, slots, acts, grads, start):
    out = (message(4 * LEN, CHUNKS[run][0]), jnp.bfloat16)
    return sums(sent_kernel, "sent_sums", run, slots, acts, grads, start, out)


def kept_sums(run, slots, acts, grads, start):
    out = ((4 * LEN, CHUNKS[run][0]), jnp.float32)
    return sums(kept_kernel, "kept_sums", run, slots, acts, grads, start, out)


def fold(slots, mine, received):
    rows, features = mine.shape[0] // 2, mine.shape[1]
    outs = (
        ((rows, features), jnp.float32),
        (message(rows, features), jnp.bfloat16),
    )
    return call(fold_kernel, "fold", features, slots, [(mine, 0), (received, 0)], outs, 1)


def final(mine, received, start, total, before):
    first = start // TILE
    ins = (mine, received) if before is None else (mine, received, before)
    specs = [
        pl.BlockSpec((LEN, TILE), lambda i: (0, i)),
        pl.BlockSpec((1,) + received.shape[1:], lambda i: (i, 0, 0)),
        pl.BlockSpec(memory_space=pl.ANY),
    ]
    return pl.pallas_call(
        final_kernel,
        name="final",
        grid=(mine.shape[1] // TILE,),
        in_specs=specs[: len(ins)],
        out_specs=pl.BlockSpec((TILE, LEN), lambda i: (i + first, 0)),
        out_shape=jax.ShapeDtypeStruct((total, LEN), jnp.float32),
        input_output_aliases={} if before is None else {2: 0},
        compiler_params=pltpu.CompilerParams(vmem_limit_bytes=VMEM),
    )(*ins)


def per_device(activations, out_grads):
    dp, tensor = lax.axis_index("dp"), lax.axis_index("tensor")
    z_lo, x, y = dp // (NX * NY), (dp // NY) % NX, dp % NY
    z_hi, core = tensor // 2, tensor % 2

    def slots_of(order):
        slots = []
        for n in range(8):
            bits = {d: (n >> (2 - i)) & 1 for i, d in enumerate(order)}
            wanted = (z_lo ^ bits["z"]) * NX + (x ^ bits["a"] ^ (3 * bits["b"]))
            slots.append(((wanted // 2 - z_hi) % NZ) * 2 + (wanted + core) % 2)
        return slots

    slots = [slot for _, order in CHUNKS for slot in slots_of(order)]
    slots = jnp.stack(slots).astype(jnp.int32)
    turned = out_grads.T
    width = turned.shape[0] // NY

    def block_for(offset):
        start = ((y + offset) % NY) * width
        return lax.dynamic_slice_in_dim(turned, start, width, axis=0)

    mine = jnp.stack([block_for(0)] + [from_y(block_for(-o), o) for o in range(1, NY)])
    mine, slots = lax.optimization_barrier((mine, slots))
    after_y, before_y = from_y(activations, 1), from_y(activations, -1)
    z_up, z_down = from_z(mine, 1), from_z(mine, -1)
    other_mine = from_core(mine)
    near = jnp.stack([z_up, z_down])
    far = jnp.concatenate([from_z(near[1, :2], -1), from_z(near[0, 2:], 1)])
    far_a, far_b = from_y(before_y[:LEN], -1), from_y(after_y[LEN:], 1)
    other_near = from_core(near)
    far = after(far, far_a, far_b)
    other_far = from_core(far)
    grads = jnp.stack(
        [mine, other_mine, near[0], other_near[0]]
        + [far, other_far, near[1], other_near[1]]
    )
    acts = (activations, after_y, far_a, far_b, before_y)

    starts = [sum(f for f, _ in CHUNKS[:n]) for n in range(len(CHUNKS))]
    start = sum(f for f, _ in CHUNKS)
    received, kept = {}, {}
    for run, (_, order) in enumerate(CHUNKS):
        sent = sent_sums(run, slots, acts, grads, starts[run])
        received[run] = swap(sent, **FOLDS[order[0]])
        slots = after(slots, sent)

    def keep(run, slots):
        kept[run] = kept_sums(run, slots, acts, grads, starts[run])
        return after(slots, kept[run])

    slots = keep(1, keep(0, slots))
    for step in (1, 2):
        for run, (_, order) in enumerate(CHUNKS):
            kept[run], sent = fold(slots, kept[run], received[run])
            received[run] = swap(sent, **FOLDS[order[step]])
            slots = after(slots, kept[run])
            if run + 2 < len(CHUNKS) and step == 1:
                slots = keep(run + 2, slots)
    runs = [(starts[n], None, kept[n], received[n]) for n in range(len(CHUNKS))]
    result = None
    for first, _, kept, received in runs:
        result = final(kept, received, first, start, result)
    return result


def solution(mesh):
    in_specs = (P("dp", "tensor"), P("dp", "tensor"))
    out_specs = P("tensor", "dp")
    return jax.shard_map(
        per_device, mesh=mesh, in_specs=in_specs, out_specs=out_specs, check_vma=False
    )
```

```python
import functools

import jax
import jax.numpy as jnp
from jax import lax
from jax.experimental import pallas as pl
from jax.experimental.pallas import tpu as pltpu
from jax.sharding import PartitionSpec as P

LEN = 128
NX, NY, NZ = 4, 4, 4
TILE = 256
LANES = 128
CHUNKS = ((512, "abz"), (512, "baz"), (512, "zab"), (256, "abz"))
CODE_TOP = 2.0**14
LEAST = 2.0**-120
VMEM = 16 * 1024 * 1024


def dp_index(z, x, y):
    return (z % 2) * NX * NY + (x % NX) * NY + (y % NY)


def swap(array, z=0, x=0, y=0):
    pairs = [
        (dp_index(k, i, j), dp_index(k ^ z, i ^ x, j ^ y))
        for k in range(2)
        for i in range(NX)
        for j in range(NY)
    ]
    return lax.ppermute(array, "dp", pairs)


FOLDS = {"z": {"z": 1}, "a": {"x": 1}, "b": {"x": 3}}


def tensor_moves(dz, flip):
    return [
        (2 * z + c, 2 * ((z + dz) % NZ) + (c ^ flip))
        for z in range(NZ)
        for c in range(2)
    ]


def from_y(array, offset):
    pairs = [
        (dp_index(k, i, j), dp_index(k, i, j - offset))
        for k in range(2)
        for i in range(NX)
        for j in range(NY)
    ]
    return lax.ppermute(array, "dp", pairs)


def from_z(array, offset):
    return lax.ppermute(array, "tensor", tensor_moves(-offset, 0))


def from_core(array):
    return lax.ppermute(array, "tensor", tensor_moves(0, 1))


def after(later, *earlier):
    return lax.optimization_barrier((later, *earlier))[0]


def put(ref, parts, tile=0):
    pieces = [p[:, n : n + LANES] for p in parts for n in range(0, TILE, LANES)]
    tops = [jnp.max(p, axis=0, keepdims=True) for p in pieces]
    top = functools.reduce(jnp.maximum, tops)
    top = jnp.maximum(top, LEAST).astype(jnp.bfloat16).astype(jnp.float32)
    inverse = 1.0 / top
    row = 0
    for piece in pieces:
        scaled = piece * inverse * CODE_TOP
        scaled = scaled * scaled
        scaled = scaled * scaled
        scaled = scaled * scaled
        ref[tile, row : row + piece.shape[0], :] = scaled.astype(jnp.bfloat16)
        row += piece.shape[0]
    ref[tile, row:, :] = jnp.broadcast_to(top, (16, LANES)).astype(jnp.bfloat16)


def get(ref, start, rows, tile=0):
    scale = ref[tile, -16:, :].astype(jnp.float32)[:1] * (1.0 / CODE_TOP)
    found = []
    for n in range(TILE // LANES):
        code = ref[tile, start + n * rows : start + (n + 1) * rows, :]
        value = jnp.maximum(code.astype(jnp.float32), 2.0**-126)
        found.append(jnp.exp(jnp.log(value) * 0.125) * scale)
    return jnp.concatenate(found, axis=1)


def message(rows, features):
    return (features // TILE, rows * (TILE // LANES) + 16, LANES)


def squares(slot, grads, acts):
    own, after_y, far_a, far_b, before_y = acts
    total = None
    for e, pair in enumerate(
        (
            (own[:LEN, :], own[LEN:, :]),
            (after_y[:LEN, :], after_y[LEN:, :]),
            (far_a[...], far_b[...]),
            (before_y[:LEN, :], before_y[LEN:, :]),
        )
    ):
        for s in range(2):
            found = jnp.dot(
                grads[slot, e, :, s * LEN : (s + 1) * LEN],
                pair[s],
                preferred_element_type=jnp.float32,
            )
            total = found * found if total is None else total + found * found
    return total


def sent_kernel(run, slots, *refs):
    *acts, grads, sent = refs
    put(sent, [squares(slots[8 * run + n], grads, acts) for n in range(4, 8)])


def kept_kernel(run, slots, *refs):
    *acts, grads, kept = refs
    for n in range(4):
        block = squares(slots[8 * run + n], grads, acts)
        kept[n * LEN : (n + 1) * LEN, :] = block


def fold_kernel(slots, mine, received, kept, sent):
    half = kept.shape[0] // LEN
    rows = LEN * (TILE // LANES)
    for tile in range(kept.shape[1] // TILE):
        at = slice(tile * TILE, (tile + 1) * TILE)

        def block(n):
            own = mine[n * LEN : (n + 1) * LEN, at]
            return own + get(received, n * rows, LEN, tile)

        put(sent, [block(n) for n in range(half, 2 * half)], tile)
        for n in range(half):
            kept[n * LEN : (n + 1) * LEN, at] = block(n)


def final_kernel(mine, received, *refs):
    refs[-1][...] = (mine[...] + get(received, 0, LEN)).T


def spec_of(shape, start):
    if len(shape) == 3:
        return pl.BlockSpec((1,) + shape[1:], lambda i, s: (i, 0, 0))
    return pl.BlockSpec((shape[0], TILE), lambda i, s: (0, i + start))


def call(body, name, features, scalars, ins, outs, cost):
    return pl.pallas_call(
        body,
        name=name,
        grid_spec=pltpu.PrefetchScalarGridSpec(
            num_scalar_prefetch=1,
            grid=(features // TILE,),
            in_specs=[
                pl.BlockSpec(a.shape, lambda i, s: (0, 0, 0, 0))
                if a.ndim == 4
                else spec_of(a.shape, start)
                for a, start in ins
            ],
            out_specs=[spec_of(shape, 0) for shape, _ in outs],
        ),
        out_shape=[jax.ShapeDtypeStruct(shape, dtype) for shape, dtype in outs],
        compiler_params=pltpu.CompilerParams(vmem_limit_bytes=VMEM),
        cost_estimate=pl.CostEstimate(
            flops=cost, bytes_accessed=1, transcendentals=0
        ),
    )(scalars, *[a for a, _ in ins])


def sums(body, name, run, slots, acts, grads, start, out):
    features = CHUNKS[run][0]
    ins = [(a, start // TILE) for a in acts] + [(grads, 0)]
    cost = 1024 * 1024 * features
    body = functools.partial(body, run)
    return call(body, name, features, slots, ins, (out,), cost)[0]


def sent_sums(run, slots, acts, grads, start):
    out = (message(4 * LEN, CHUNKS[run][0]), jnp.bfloat16)
    return sums(sent_kernel, "sent_sums", run, slots, acts, grads, start, out)


def kept_sums(run, slots, acts, grads, start):
    out = ((4 * LEN, CHUNKS[run][0]), jnp.float32)
    return sums(kept_kernel, "kept_sums", run, slots, acts, grads, start, out)


def held(array):
    return pltpu.with_memory_space_constraint(array, pltpu.VMEM)


def fold(slots, mine, received):
    rows, features = mine.shape[0] // 2, mine.shape[1]
    space = pl.BlockSpec(memory_space=pltpu.VMEM)
    return pl.pallas_call(
        fold_kernel,
        name="fold",
        in_specs=[pl.BlockSpec(memory_space=pltpu.SMEM), space, space],
        out_specs=[space, space],
        out_shape=[
            pltpu.VMEM((rows, features), jnp.float32),
            pltpu.VMEM(message(rows, features), jnp.bfloat16),
        ],
        compiler_params=pltpu.CompilerParams(vmem_limit_bytes=VMEM),
        cost_estimate=pl.CostEstimate(flops=1, bytes_accessed=1, transcendentals=0),
    )(slots, held(mine), held(received))


def final(mine, received, start, total, before):
    first = start // TILE
    ins = (mine, received) if before is None else (mine, received, before)
    specs = [
        pl.BlockSpec((LEN, TILE), lambda i: (0, i)),
        pl.BlockSpec((1,) + received.shape[1:], lambda i: (i, 0, 0)),
        pl.BlockSpec(memory_space=pl.ANY),
    ]
    return pl.pallas_call(
        final_kernel,
        name="final",
        grid=(mine.shape[1] // TILE,),
        in_specs=specs[: len(ins)],
        out_specs=pl.BlockSpec((TILE, LEN), lambda i: (i + first, 0)),
        out_shape=jax.ShapeDtypeStruct((total, LEN), jnp.float32),
        input_output_aliases={} if before is None else {2: 0},
        compiler_params=pltpu.CompilerParams(vmem_limit_bytes=VMEM),
    )(*ins)


def per_device(activations, out_grads):
    dp, tensor = lax.axis_index("dp"), lax.axis_index("tensor")
    z_lo, x, y = dp // (NX * NY), (dp // NY) % NX, dp % NY
    z_hi, core = tensor // 2, tensor % 2

    def slots_of(order):
        slots = []
        for n in range(8):
            bits = {d: (n >> (2 - i)) & 1 for i, d in enumerate(order)}
            wanted = (z_lo ^ bits["z"]) * NX + (x ^ bits["a"] ^ (3 * bits["b"]))
            slots.append(((wanted // 2 - z_hi) % NZ) * 2 + (wanted + core) % 2)
        return slots

    slots = [slot for _, order in CHUNKS for slot in slots_of(order)]
    slots = jnp.stack(slots).astype(jnp.int32)
    turned = out_grads.T
    width = turned.shape[0] // NY

    def block_for(offset):
        start = ((y + offset) % NY) * width
        return lax.dynamic_slice_in_dim(turned, start, width, axis=0)

    mine = jnp.stack([block_for(0)] + [from_y(block_for(-o), o) for o in range(1, NY)])
    mine, slots = lax.optimization_barrier((mine, slots))
    after_y, before_y = from_y(activations, 1), from_y(activations, -1)
    z_up, z_down = from_z(mine, 1), from_z(mine, -1)
    other_mine = from_core(mine)
    near = jnp.stack([z_up, z_down])
    far = jnp.concatenate([from_z(near[1, :2], -1), from_z(near[0, 2:], 1)])
    far_a, far_b = from_y(before_y[:LEN], -1), from_y(after_y[LEN:], 1)
    other_near = from_core(near)
    far = after(far, far_a, far_b)
    other_far = from_core(far)
    grads = jnp.stack(
        [mine, other_mine, near[0], other_near[0]]
        + [far, other_far, near[1], other_near[1]]
    )
    acts = (activations, after_y, far_a, far_b, before_y)

    starts = [sum(f for f, _ in CHUNKS[:n]) for n in range(len(CHUNKS))]
    start = sum(f for f, _ in CHUNKS)
    received, kept = {}, {}
    for run, (_, order) in enumerate(CHUNKS):
        sent = sent_sums(run, slots, acts, grads, starts[run])
        received[run] = swap(sent, **FOLDS[order[0]])
        slots = after(slots, sent)

    def keep(run, slots):
        kept[run] = kept_sums(run, slots, acts, grads, starts[run])
        return after(slots, kept[run])

    slots = keep(1, keep(0, slots))
    for step in (1, 2):
        for run, (_, order) in enumerate(CHUNKS):
            kept[run], sent = fold(slots, kept[run], received[run])
            received[run] = swap(sent, **FOLDS[order[step]])
            slots = after(slots, kept[run])
            if run + 2 < len(CHUNKS) and step == 1:
                slots = keep(run + 2, slots)
    runs = [(starts[n], None, kept[n], received[n]) for n in range(len(CHUNKS))]
    result = None
    for first, _, kept, received in runs:
        result = final(kept, received, first, start, result)
    return result


def solution(mesh):
    in_specs = (P("dp", "tensor"), P("dp", "tensor"))
    out_specs = P("tensor", "dp")
    return jax.shard_map(
        per_device, mesh=mesh, in_specs=in_specs, out_specs=out_specs, check_vma=False
    )
```
